32 devices in a mesh: groups: 2 (over x), heads: 16 (over z, y, core).
Axes of the slice: x: 2, y: 2, z: 4, core: 2. Of those that a mesh axis runs over, the one named last changes fastest.
Arguments:
- hidden: bfloat16 [384, 6144], P('groups'), parts along dimension 0, may hold values from -6 to 6
- in_gain: float32 [1, 6144], replicated, may hold values from 0.1 to 1.9
- w_in: bfloat16 [1, 6144, 32768], P(None, 'heads'), may hold values from -0.078125 to 0.078125
- attn_gain: float32 [1, 8192], P(None, 'heads'), may hold values from 0.1 to 1.9
- w_out: bfloat16 [1, 8192, 6144], P(None, None, 'heads'), may hold values from -0.0625 to 0.0625
- slope_index: int32 [1, 64], P(None, 'heads'), may hold values from 8 to 29
Outputs:
- result: bfloat16 [384, 6144], P('groups'), parts along dimension 0
The draws below stay inside these ranges and needn't reach their ends.
There are 2 independent parts, one for each index of `groups`. The reference program is written for one: setup_inputs(seed, part) draws one part's arguments, and reference() takes and returns one part's arrays. A program takes and returns all parts, laid end to end along the dimension named above; an argument that names none is the same for every part. Nothing has to cross between parts.
All inputs are finite; a program needn't handle non-finite values.
Results may differ from the reference program's by a relative error of at most 0.0038.
Values may be sent and summed in bfloat16 or wider, within the bound.
A program may use at most 192 MiB of HBM per device.

```python
import jax
import jax.numpy as jnp
from jax import lax

D = 6144
HEADS = 64
HEAD_DIM = 128
LAYERS = 1
TOKENS = 192
ATT = 8192


def with_ends(values, key, least, high):
    place = [jax.random.randint(jax.random.fold_in(key, axis), (), 0, length) for axis, length in enumerate(values.shape)]
    longest = values.shape.index(max(values.shape))
    next_to = place[:longest] + [(place[longest] + 1) % values.shape[longest]] + place[longest + 1:]
    return values.at[tuple(place)].set(least).at[tuple(next_to)].set(high)


def block_levels(stream_key, dims, pieces, low, high):
    def one(dim, shards_of):
        heights = jax.random.uniform(jax.random.fold_in(jax.random.fold_in(stream_key, 6), dim), (shards_of,), jnp.float32, low / len(pieces), high / len(pieces))
        return jnp.repeat(jnp.exp(heights), dims[dim] // shards_of).reshape((-1,) + (1,) * (len(dims) - dim - 1))

    gain = one(*pieces[0])
    for cut in pieces[1:]:
        gain = gain * one(*cut)
    return gain


def gaussian(stream_key, extent, scale, bound, split=(), held_as=jnp.bfloat16):
    values = scale * jax.random.normal(stream_key, extent, jnp.float32)
    if split:
        values = values * block_levels(stream_key, extent, split, -0.22, 0.18)
    return jnp.clip(values, -bound, bound).astype(held_as)


def setup_inputs(seed: int = 0, part: int = 0) -> dict:
    key_of = jax.random.split(jax.random.key(seed), 7)
    part_keys = jax.random.split(jax.random.fold_in(key_of[6], part), 7)
    return {
        "hidden": gaussian(part_keys[0], (TOKENS, D), 1.0, 6.0),
        "in_gain": jnp.clip(1.0 + 0.18 * jax.random.normal(key_of[1], (LAYERS, D), jnp.float32), 0.1, 1.9),
        "w_in": gaussian(key_of[2], (LAYERS, D, 4 * ATT), D ** -0.5, 0.078125, ((1, 16),)),
        "attn_gain": jnp.clip(1.0 + 0.18 * jax.random.normal(key_of[3], (LAYERS, ATT), jnp.float32), 0.1, 1.9),
        "w_out": gaussian(key_of[4], (LAYERS, ATT, D), ATT ** -0.5, 0.0625, ((2, 16),)),
        "slope_index": with_ends(jax.random.randint(key_of[5], (LAYERS, HEADS), 8, 30), jax.random.fold_in(key_of[5], 1), 8, 29).astype(jnp.int32),
    }


def decay_weights(query_head, key_head, slope):
    scores = jnp.dot(query_head, key_head.T, preferred_element_type=jnp.float32)
    positions = jnp.arange(TOKENS, dtype=jnp.int32)
    offset = (positions[:, None] - positions[None, :]).astype(jnp.float32)
    decay = jnp.where(offset >= 0.0, jnp.exp(-slope * jnp.maximum(offset, 0.0)), 0.0)
    return (scores * decay).astype(jnp.bfloat16)

def one_head(inputs):
    query_head, key_head, value_head, slope = inputs
    weights = decay_weights(query_head, key_head, slope)
    return jnp.dot(weights, value_head, preferred_element_type=jnp.float32)

def split_heads(block):
    return block.reshape(TOKENS, HEADS, HEAD_DIM).transpose(1, 0, 2)

def reference(hidden, in_gain, w_in, attn_gain, w_out, slope_index):
    stream = hidden
    for layer_index in range(LAYERS):
        widened = stream.astype(jnp.float32)
        scale = lax.rsqrt(lax.optimization_barrier(jnp.mean(widened * widened, axis=1, keepdims=True)) + 1e-06)
        normed = (widened * scale * in_gain[layer_index][None, :]).astype(jnp.bfloat16)
        proj = jnp.dot(normed, w_in[layer_index], preferred_element_type=jnp.float32)
        query = jax.nn.silu(proj[:, :ATT]).astype(jnp.bfloat16)
        keys = jax.nn.silu(proj[:, ATT:2 * ATT]).astype(jnp.bfloat16)
        values = jax.nn.silu(proj[:, 2 * ATT:3 * ATT]).astype(jnp.bfloat16)
        gate = proj[:, 3 * ATT:]
        slopes = jnp.exp2(-0.5 * slope_index[layer_index].astype(jnp.float32))
        attn = lax.map(one_head, (split_heads(query), split_heads(keys), split_heads(values), slopes))
        attn = attn.transpose(1, 0, 2).reshape(TOKENS, ATT)
        total = lax.optimization_barrier(jnp.sum(attn * attn, axis=1, keepdims=True))
        mixed = (attn * lax.rsqrt(total / ATT + 1e-06) * attn_gain[layer_index][None, :] * jax.nn.sigmoid(gate)).astype(jnp.bfloat16)
        projected = jnp.dot(mixed, w_out[layer_index], preferred_element_type=jnp.float32)
        stream = (widened + projected).astype(jnp.bfloat16)
    return stream
```

```python
import jax
import jax.numpy as jnp
from jax import lax
from jax.sharding import PartitionSpec as P

D = 6144


def on_device(hidden, in_gain, w_in, attn_gain, w_out, slope_index):
    members = lax.axis_size("heads")
    position = lax.axis_index("heads")
    shard_rows = w_in.shape[1]
    columns = attn_gain.shape[1]
    heads_local = slope_index.shape[1]
    head_width = columns // heads_local
    attn_width = columns * members
    out_columns = w_out.shape[2]
    widened = hidden.astype(jnp.float32)
    tokens = widened.shape[0]

    scale = lax.rsqrt(jnp.mean(widened * widened, axis=1, keepdims=True) + 1e-06)
    own_hidden = lax.dynamic_slice_in_dim(hidden, position * shard_rows, shard_rows, 1)
    own_gain = lax.dynamic_slice_in_dim(in_gain, position * shard_rows, shard_rows, 1)
    normed = (own_hidden.astype(jnp.float32) * scale * own_gain).astype(jnp.bfloat16)

    partial = jnp.dot(normed, w_in[0], preferred_element_type=jnp.float32).astype(jnp.bfloat16)
    partial = partial.reshape(tokens, 4, members, columns).transpose(2, 0, 1, 3)
    proj = lax.psum_scatter(partial, "heads", scatter_dimension=0, tiled=False)
    proj = proj.astype(jnp.float32)

    query = jax.nn.silu(proj[:, 0]).astype(jnp.bfloat16).reshape(tokens, heads_local, head_width)
    keys = jax.nn.silu(proj[:, 1]).astype(jnp.bfloat16).reshape(tokens, heads_local, head_width)
    values = jax.nn.silu(proj[:, 2]).astype(jnp.bfloat16).reshape(tokens, heads_local, head_width)
    gate = proj[:, 3]
    slopes = jnp.exp2(-0.5 * slope_index[0].astype(jnp.float32))
    positions = jnp.arange(tokens, dtype=jnp.int32)
    offset = (positions[:, None] - positions[None, :]).astype(jnp.float32)
    decay = jnp.where(
        offset[None] >= 0.0, jnp.exp(-slopes[:, None, None] * jnp.maximum(offset, 0.0)[None]), 0.0
    )
    scores = jnp.einsum("thd,shd->hts", query, keys, preferred_element_type=jnp.float32)
    weights = (scores * decay).astype(jnp.bfloat16)
    attn = jnp.einsum("hts,shd->thd", weights, values, preferred_element_type=jnp.float32).reshape(
        tokens, columns
    )
    total = lax.psum(jnp.sum(attn * attn, axis=1), "heads")
    mixed = (
        attn
        * lax.rsqrt(total[:, None] / attn_width + 1e-06)
        * attn_gain[0][None, :]
        * jax.nn.sigmoid(gate)
    ).astype(jnp.bfloat16)

    mixed_all = lax.all_gather(mixed, "heads", axis=0, tiled=False)
    w_blocks = w_out[0].reshape(members, columns, out_columns)
    update = jnp.einsum("mtc,mcd->td", mixed_all, w_blocks, preferred_element_type=jnp.float32)
    own = lax.dynamic_slice_in_dim(hidden, position * out_columns, out_columns, 1)
    updated = (own.astype(jnp.float32) + update).astype(jnp.bfloat16)
    return lax.all_gather(updated, "heads", axis=1, tiled=True)


def solution(mesh):
    placed = (
        P("groups", None),
        P(),
        P(None, "heads", None),
        P(None, "heads"),
        P(None, None, "heads"),
        P(None, "heads"),
    )
    return jax.shard_map(
        on_device, mesh=mesh, in_specs=placed, out_specs=P("groups", None), check_vma=False
    )
```

```python
import functools

import jax
import jax.numpy as jnp
from jax import lax
from jax.experimental import pallas as pl
from jax.experimental.pallas import tpu as pltpu
from jax.sharding import PartitionSpec as P

KINDS = 4
W_PARTS = 4


def bit_orders(steps):
    forward = tuple(range(steps))
    turned = (0,) + tuple(range(2, steps)) + (1,)
    return (forward, turned, forward, forward)


def project_kernel(members, normed_ref, w_ref, out_ref, w_buf, part, got, w_sem, send_sem, recv_sem):
    me = lax.axis_index("heads")
    steps = members.bit_length() - 1
    columns = out_ref.shape[2]
    orders = bit_orders(steps)
    width = members * columns

    def my_bit(bit):
        return lax.rem(me // (1 << bit), 2)

    def partner(bit):
        return me + (1 - 2 * my_bit(bit)) * (1 << bit)

    def w_copy(kind, piece):
        length = width // W_PARTS
        return pltpu.make_async_copy(
            w_ref.at[:, pl.ds(kind * width + piece * length, length)],
            w_buf.at[kind % 2, :, pl.ds(piece * length, length)],
            w_sem.at[kind, piece],
        )

    def w_start(kind):
        for piece in range(W_PARTS):
            w_copy(kind, piece).start()

    w_start(0)
    w_start(1)

    barrier = pltpu.get_barrier_semaphore()
    for bit in range(steps):
        pl.semaphore_signal(barrier, inc=1, device_id={"heads": partner(bit)})
    pl.semaphore_wait(barrier, steps)

    def multiply(kind):
        for piece in range(W_PARTS):
            w_copy(kind, piece).wait()

        @pl.loop(0, members)
        def _(place):
            owner = 0
            for step, bit in enumerate(orders[kind]):
                owner = owner + lax.rem(place // (1 << (steps - 1 - step)), 2) * (1 << bit)
            begin = pl.multiple_of(owner * columns, columns)
            block = jnp.dot(
                normed_ref[...],
                w_buf[kind % 2, :, pl.ds(begin, columns)],
                preferred_element_type=jnp.float32,
            )
            part[kind, place] = block.astype(part.dtype)

        if kind + 2 < KINDS:
            w_start(kind + 2)

    def layout(kind, step):
        base = 0
        for earlier in range(step):
            base = base + my_bit(orders[kind][earlier]) * (members >> (earlier + 1))
        length = members >> (step + 1)
        bit = orders[kind][step]
        keep = base + my_bit(bit) * length
        give = base + (1 - my_bit(bit)) * length
        return length, keep, give, members - (members >> step)

    def remote(kind, step):
        length, _, give, at = layout(kind, step)
        return pltpu.make_async_remote_copy(
            src_ref=part.at[kind, pl.ds(give, length)],
            dst_ref=got.at[kind, pl.ds(at, length)],
            send_sem=send_sem.at[kind, step],
            recv_sem=recv_sem.at[kind, step],
            device_id={"heads": partner(orders[kind][step])},
        )

    def send(kind, step):
        remote(kind, step).start()

    def arrive(kind, step):
        remote(kind, step).wait_recv()

    def add(kind, step):
        length, keep, _, at = layout(kind, step)
        if length == 1:
            out_ref[kind] = part[kind, keep].astype(jnp.float32) + got[kind, at].astype(jnp.float32)
            return

        @pl.loop(0, length)
        def _(index):
            total = part[kind, keep + index].astype(jnp.float32) + got[kind, at + index].astype(
                jnp.float32
            )
            part[kind, keep + index] = total.astype(part.dtype)

    multiply(0)
    send(0, 0)
    multiply(1)
    send(1, 0)
    arrive(0, 0)
    add(0, 0)
    send(0, 1)
    multiply(2)
    send(2, 0)
    arrive(1, 0)
    add(1, 0)
    send(1, 1)
    multiply(3)
    send(3, 0)
    arrive(2, 0)
    add(2, 0)
    arrive(3, 0)
    add(3, 0)
    arrive(0, 1)
    send(2, 1)
    add(0, 1)
    send(0, 2)
    arrive(1, 1)
    add(1, 1)
    send(1, 2)
    arrive(0, 2)
    add(0, 2)
    if steps > 3:
        send(0, 3)
    arrive(2, 1)
    send(3, 1)
    add(2, 1)
    send(2, 2)
    sent = {(0, s) for s in range(4)} | {(1, s) for s in range(3)} | {(2, s) for s in range(3)}
    sent |= {(3, 0), (3, 1)}
    taken = {(0, s) for s in range(3)} | {(1, 0), (1, 1), (2, 0), (2, 1), (3, 0)}
    for step in range(1, steps):
        for kind in (1, 2, 0, 3):
            if (kind, step) in taken:
                continue
            arrive(kind, step)
            add(kind, step)
            if step + 1 < steps and (kind, step + 1) not in sent:
                send(kind, step + 1)
    for kind in range(KINDS):
        for step in range(steps):
            remote(kind, step).wait_send()


def project(members, columns, normed, w_in):
    tokens, rows = normed.shape
    steps = members.bit_length() - 1
    return pl.pallas_call(
        functools.partial(project_kernel, members),
        out_shape=jax.ShapeDtypeStruct((KINDS, tokens, columns), jnp.float32),
        in_specs=[
            pl.BlockSpec(memory_space=pltpu.VMEM),
            pl.BlockSpec(memory_space=pl.ANY),
        ],
        out_specs=pl.BlockSpec(memory_space=pltpu.VMEM),
        scratch_shapes=[
            pltpu.VMEM((2, rows, members * columns), jnp.bfloat16),
            pltpu.VMEM((KINDS, members, tokens, columns), jnp.bfloat16),
            pltpu.VMEM((KINDS, members - 1, tokens, columns), jnp.bfloat16),
            pltpu.SemaphoreType.DMA((KINDS, W_PARTS)),
            pltpu.SemaphoreType.DMA((KINDS, steps)),
            pltpu.SemaphoreType.DMA((KINDS, steps)),
        ],
        compiler_params=pltpu.CompilerParams(
            collective_id=0, has_side_effects=True, vmem_limit_bytes=56 * 1024 * 1024
        ),
        cost_estimate=pl.CostEstimate(
            flops=2 * tokens * rows * KINDS * members * columns,
            bytes_accessed=2 * rows * KINDS * members * columns,
            transcendentals=0,
        ),
    )(normed, w_in)


def on_device(hidden, in_gain, w_in, attn_gain, w_out, slope_index):
    members = lax.axis_size("heads")
    position = lax.axis_index("heads")
    shard_rows = w_in.shape[1]
    columns = attn_gain.shape[1]
    heads_local = slope_index.shape[1]
    head_width = columns // heads_local
    attn_width = columns * members
    out_columns = w_out.shape[2]
    widened = hidden.astype(jnp.float32)
    tokens = widened.shape[0]

    scale = lax.rsqrt(jnp.mean(widened * widened, axis=1, keepdims=True) + 1e-06)
    own_hidden = lax.dynamic_slice_in_dim(hidden, position * shard_rows, shard_rows, 1)
    own_gain = lax.dynamic_slice_in_dim(in_gain, position * shard_rows, shard_rows, 1)
    normed = (own_hidden.astype(jnp.float32) * scale * own_gain).astype(jnp.bfloat16)

    proj = project(members, columns, normed, w_in[0])

    query = jax.nn.silu(proj[0]).astype(jnp.bfloat16).reshape(tokens, heads_local, head_width)
    keys = jax.nn.silu(proj[1]).astype(jnp.bfloat16).reshape(tokens, heads_local, head_width)
    values = jax.nn.silu(proj[2]).astype(jnp.bfloat16).reshape(tokens, heads_local, head_width)
    gate = proj[3]
    slopes = jnp.exp2(-0.5 * slope_index[0].astype(jnp.float32))
    positions = jnp.arange(tokens, dtype=jnp.int32)
    offset = (positions[:, None] - positions[None, :]).astype(jnp.float32)
    decay = jnp.where(
        offset[None] >= 0.0, jnp.exp(-slopes[:, None, None] * jnp.maximum(offset, 0.0)[None]), 0.0
    )
    scores = jnp.einsum("thd,shd->hts", query, keys, preferred_element_type=jnp.float32)
    weights = (scores * decay).astype(jnp.bfloat16)
    attn = jnp.einsum("hts,shd->thd", weights, values, preferred_element_type=jnp.float32).reshape(
        tokens, columns
    )
    total = lax.psum(jnp.sum(attn * attn, axis=1), "heads")
    mixed = (
        attn
        * lax.rsqrt(total[:, None] / attn_width + 1e-06)
        * attn_gain[0][None, :]
        * jax.nn.sigmoid(gate)
    ).astype(jnp.bfloat16)

    mixed_all = lax.all_gather(mixed, "heads", axis=0, tiled=False)
    w_blocks = w_out[0].reshape(members, columns, out_columns)
    update = jnp.einsum("mtc,mcd->td", mixed_all, w_blocks, preferred_element_type=jnp.float32)
    own = lax.dynamic_slice_in_dim(hidden, position * out_columns, out_columns, 1)
    updated = (own.astype(jnp.float32) + update).astype(jnp.bfloat16)
    return lax.all_gather(updated, "heads", axis=1, tiled=True)


def solution(mesh):
    placed = (
        P("groups", None),
        P(),
        P(None, "heads", None),
        P(None, "heads"),
        P(None, None, "heads"),
        P(None, "heads"),
    )
    return jax.shard_map(
        on_device, mesh=mesh, in_specs=placed, out_specs=P("groups", None), check_vma=False
    )
```

```python
import functools

import jax
import jax.numpy as jnp
from jax import lax
from jax.experimental import pallas as pl
from jax.experimental.pallas import tpu as pltpu
from jax.sharding import PartitionSpec as P

KINDS = 4
W_PARTS = 4


def bit_orders(steps):
    forward = tuple(range(steps))
    turned = (0,) + tuple(range(2, steps)) + (1,)
    return (forward, turned, forward, forward)


def project_kernel(members, normed_ref, w_ref, out_ref, w_buf, part, got, w_sem, send_sem, recv_sem):
    me = lax.axis_index("heads")
    steps = members.bit_length() - 1
    columns = out_ref.shape[2]
    orders = bit_orders(steps)
    width = members * columns

    def my_bit(bit):
        return lax.rem(me // (1 << bit), 2)

    def partner(bit):
        return me + (1 - 2 * my_bit(bit)) * (1 << bit)

    def w_copy(kind, piece):
        length = width // W_PARTS
        return pltpu.make_async_copy(
            w_ref.at[:, pl.ds(kind * width + piece * length, length)],
            w_buf.at[kind % 2, :, pl.ds(piece * length, length)],
            w_sem.at[kind, piece],
        )

    def w_start(kind):
        for piece in range(W_PARTS):
            w_copy(kind, piece).start()

    w_start(0)
    w_start(1)

    barrier = pltpu.get_barrier_semaphore()
    for bit in range(steps):
        pl.semaphore_signal(barrier, inc=1, device_id={"heads": partner(bit)})
    pl.semaphore_wait(barrier, steps)

    def multiply(kind):
        for piece in range(W_PARTS):
            w_copy(kind, piece).wait()

        @pl.loop(0, members)
        def _(place):
            owner = 0
            for step, bit in enumerate(orders[kind]):
                owner = owner + lax.rem(place // (1 << (steps - 1 - step)), 2) * (1 << bit)
            begin = pl.multiple_of(owner * columns, columns)
            block = jnp.dot(
                normed_ref[...],
                w_buf[kind % 2, :, pl.ds(begin, columns)],
                preferred_element_type=jnp.float32,
            )
            part[kind, place] = block.astype(part.dtype)

        if kind + 2 < KINDS:
            w_start(kind + 2)

    def layout(kind, step):
        base = 0
        for earlier in range(step):
            base = base + my_bit(orders[kind][earlier]) * (members >> (earlier + 1))
        length = members >> (step + 1)
        bit = orders[kind][step]
        keep = base + my_bit(bit) * length
        give = base + (1 - my_bit(bit)) * length
        return length, keep, give, members - (members >> step)

    def remote(kind, step):
        length, _, give, at = layout(kind, step)
        return pltpu.make_async_remote_copy(
            src_ref=part.at[kind, pl.ds(give, length)],
            dst_ref=got.at[kind, pl.ds(at, length)],
            send_sem=send_sem.at[kind, step],
            recv_sem=recv_sem.at[kind, step],
            device_id={"heads": partner(orders[kind][step])},
        )

    def send(kind, step):
        remote(kind, step).start()

    def arrive(kind, step):
        remote(kind, step).wait_recv()

    def add(kind, step):
        length, keep, _, at = layout(kind, step)
        if length == 1:
            out_ref[kind] = part[kind, keep].astype(jnp.float32) + got[kind, at].astype(jnp.float32)
            return

        @pl.loop(0, length)
        def _(index):
            total = part[kind, keep + index].astype(jnp.float32) + got[kind, at + index].astype(
                jnp.float32
            )
            part[kind, keep + index] = total.astype(part.dtype)

    multiply(0)
    send(0, 0)
    multiply(1)
    send(1, 0)
    arrive(0, 0)
    add(0, 0)
    send(0, 1)
    multiply(2)
    send(2, 0)
    arrive(1, 0)
    add(1, 0)
    send(1, 1)
    multiply(3)
    send(3, 0)
    arrive(2, 0)
    add(2, 0)
    arrive(3, 0)
    add(3, 0)
    arrive(0, 1)
    send(2, 1)
    add(0, 1)
    send(0, 2)
    arrive(1, 1)
    add(1, 1)
    send(1, 2)
    arrive(0, 2)
    add(0, 2)
    if steps > 3:
        send(0, 3)
    arrive(2, 1)
    send(3, 1)
    add(2, 1)
    send(2, 2)
    sent = {(0, s) for s in range(4)} | {(1, s) for s in range(3)} | {(2, s) for s in range(3)}
    sent |= {(3, 0), (3, 1)}
    taken = {(0, s) for s in range(3)} | {(1, 0), (1, 1), (2, 0), (2, 1), (3, 0)}
    for step in range(1, steps):
        for kind in (1, 2, 0, 3):
            if (kind, step) in taken:
                continue
            arrive(kind, step)
            add(kind, step)
            if step + 1 < steps and (kind, step + 1) not in sent:
                send(kind, step + 1)
    for kind in range(KINDS):
        for step in range(steps):
            remote(kind, step).wait_send()


def project(members, columns, normed, w_in):
    tokens, rows = normed.shape
    steps = members.bit_length() - 1
    return pl.pallas_call(
        functools.partial(project_kernel, members),
        out_shape=jax.ShapeDtypeStruct((KINDS, tokens, columns), jnp.float32),
        in_specs=[
            pl.BlockSpec(memory_space=pltpu.VMEM),
            pl.BlockSpec(memory_space=pl.ANY),
        ],
        out_specs=pl.BlockSpec(memory_space=pltpu.VMEM),
        scratch_shapes=[
            pltpu.VMEM((2, rows, members * columns), jnp.bfloat16),
            pltpu.VMEM((KINDS, members, tokens, columns), jnp.bfloat16),
            pltpu.VMEM((KINDS, members - 1, tokens, columns), jnp.bfloat16),
            pltpu.SemaphoreType.DMA((KINDS, W_PARTS)),
            pltpu.SemaphoreType.DMA((KINDS, steps)),
            pltpu.SemaphoreType.DMA((KINDS, steps)),
        ],
        compiler_params=pltpu.CompilerParams(
            collective_id=0, has_side_effects=True, vmem_limit_bytes=56 * 1024 * 1024
        ),
        cost_estimate=pl.CostEstimate(
            flops=2 * tokens * rows * KINDS * members * columns,
            bytes_accessed=2 * rows * KINDS * members * columns,
            transcendentals=0,
        ),
    )(normed, w_in)


def output_kernel(
    members, attn_width, scaled_ref, squares_ref, own_ref, w_ref, out_ref,
    w_buf, mix, acc, res, tot, tot_got, w_sem, tot_sem, mix_send, mix_recv, res_send, res_recv,
):
    me = lax.axis_index("heads")
    steps = members.bit_length() - 1
    halves, _, tokens, half = mix.shape
    columns = scaled_ref.shape[1]
    res_rows = res.shape[2]
    far_bits = tuple(range(steps - 1, 1, -1))
    orders = (far_bits + (1, 0), (1,) + far_bits + (0,))

    def my_bit(bit):
        return lax.rem(me // (1 << bit), 2)

    def partner(bit):
        return me + (1 - 2 * my_bit(bit)) * (1 << bit)

    w_rows = w_ref.shape[0] // W_PARTS

    def w_copy(piece):
        rows = pl.ds(piece * w_rows, w_rows)
        return pltpu.make_async_copy(w_ref.at[rows], w_buf.at[rows], w_sem.at[piece])

    for piece in range(W_PARTS):
        w_copy(piece).start()

    barrier = pltpu.get_barrier_semaphore()
    for bit in range(steps):
        pl.semaphore_signal(barrier, inc=1, device_id={"heads": partner(bit)})
    pl.semaphore_wait(barrier, steps)

    def total_copy(step):
        return pltpu.make_async_remote_copy(
            src_ref=tot.at[step],
            dst_ref=tot_got.at[step],
            send_sem=tot_sem.at[0, step],
            recv_sem=tot_sem.at[1, step],
            device_id={"heads": partner(step)},
        )

    tot[0] = squares_ref[...]
    for step in range(steps):
        total_copy(step).start()
        total_copy(step).wait_recv()
        tot[step + 1] = tot[step] + tot_got[step]
    across = jnp.broadcast_to(tot[steps][:1], (tokens, tokens))
    diagonal = lax.broadcasted_iota(jnp.int32, (tokens, tokens), 0) == lax.broadcasted_iota(
        jnp.int32, (tokens, tokens), 1
    )
    total = jnp.sum(jnp.where(diagonal, across, 0.0), axis=1, keepdims=True)
    norm = lax.rsqrt(total / attn_width + 1e-06)

    def held(order, step):
        base = 0
        for later in range(step, steps):
            base = base + my_bit(order[later]) * (1 << later)
        return base

    def incoming(order, step):
        return held(order, step) + (1 - 2 * my_bit(order[step])) * (1 << step)

    def owner_of(order, place):
        owner = 0
        for step, bit in enumerate(order):
            owner = owner + lax.rem(place // (1 << step), 2) * (1 << bit)
        return owner

    def block_copy(buffer, sends, recvs, which, step, base):
        run = pl.ds(base, 1 << step)
        return pltpu.make_async_remote_copy(
            src_ref=buffer.at[which, run],
            dst_ref=buffer.at[which, run],
            send_sem=sends.at[which, step],
            recv_sem=recvs.at[which, step],
            device_id={"heads": partner(orders[which][step])},
        )

    def mix_start(which, step):
        block_copy(mix, mix_send, mix_recv, which, step, held(orders[which], step)).start()

    def mix_arrive(which, step):
        block_copy(mix, mix_send, mix_recv, which, step, incoming(orders[which], step)).wait_recv()

    def res_start(which, step):
        block_copy(res, res_send, res_recv, which, step, held(orders[which], step)).start()

    def res_arrive(which, step):
        block_copy(res, res_send, res_recv, which, step, incoming(orders[which], step)).wait_recv()

    def multiply(which, first, count):
        @pl.loop(0, count)
        def _(index):
            place = first + index
            begin = pl.multiple_of(owner_of(orders[which], place) * columns + which * half, half)
            acc[...] += jnp.dot(
                mix[which, place], w_buf[pl.ds(begin, half)], preferred_element_type=jnp.float32
            )

    for which in range(halves):
        lanes = slice(which * half, (which + 1) * half)
        mix[which, held(orders[which], 0)] = (scaled_ref[:, lanes] * norm).astype(mix.dtype)
        mix_start(which, 0)
    acc[...] = own_ref[...].astype(jnp.float32)
    for piece in range(W_PARTS):
        w_copy(piece).wait()
    for which in range(halves):
        multiply(which, held(orders[which], 0), 1)
    for step in range(steps):
        for which in range(halves):
            mix_arrive(which, step)
            if step + 1 < steps:
                mix_start(which, step + 1)
            multiply(which, incoming(orders[which], step), 1 << step)

    for which in range(2):
        rows = slice(which * res_rows, (which + 1) * res_rows)
        res[which, held(orders[which], 0)] = acc[rows].astype(res.dtype)
        res_start(which, 0)

    def put(which, first, count):
        @pl.loop(0, count)
        def _(index):
            place = first + index
            rows = slice(which * res_rows, (which + 1) * res_rows)
            out_ref[owner_of(orders[which], place), rows] = res[which, place]

    for which in range(2):
        put(which, held(orders[which], 0), 1)
    for step in range(steps):
        for which in range(2):
            res_arrive(which, step)
            if step + 1 < steps:
                res_start(which, step + 1)
            put(which, incoming(orders[which], step), 1 << step)

    for step in range(steps):
        total_copy(step).wait_send()
        for which in range(halves):
            block_copy(mix, mix_send, mix_recv, which, step, held(orders[which], step)).wait_send()
        for which in range(2):
            block_copy(res, res_send, res_recv, which, step, held(orders[which], step)).wait_send()


def output_rows(members, scaled, squares, own, w_out):
    tokens, columns = scaled.shape
    out_columns = own.shape[1]
    steps = members.bit_length() - 1
    halves = 2 if columns % 256 == 0 else 1
    whole = pl.BlockSpec(memory_space=pltpu.VMEM)
    blocks = pl.pallas_call(
        functools.partial(output_kernel, members, columns * members),
        out_shape=jax.ShapeDtypeStruct((members, tokens, out_columns), jnp.bfloat16),
        in_specs=[whole, whole, whole, pl.BlockSpec(memory_space=pl.ANY)],
        out_specs=whole,
        scratch_shapes=[
            pltpu.VMEM(w_out.shape, jnp.bfloat16),
            pltpu.VMEM((halves, members, tokens, columns // halves), jnp.bfloat16),
            pltpu.VMEM((tokens, out_columns), jnp.float32),
            pltpu.VMEM((2, members, tokens // 2, out_columns), jnp.bfloat16),
            pltpu.VMEM((steps + 1,) + squares.shape, jnp.float32),
            pltpu.VMEM((steps,) + squares.shape, jnp.float32),
            pltpu.SemaphoreType.DMA((W_PARTS,)),
            pltpu.SemaphoreType.DMA((2, steps)),
            pltpu.SemaphoreType.DMA((halves, steps)),
            pltpu.SemaphoreType.DMA((halves, steps)),
            pltpu.SemaphoreType.DMA((2, steps)),
            pltpu.SemaphoreType.DMA((2, steps)),
        ],
        compiler_params=pltpu.CompilerParams(
            collective_id=1, has_side_effects=True, vmem_limit_bytes=48 * 1024 * 1024
        ),
        cost_estimate=pl.CostEstimate(
            flops=2 * tokens * w_out.shape[0] * out_columns,
            bytes_accessed=2 * w_out.shape[0] * out_columns,
            transcendentals=0,
        ),
    )(scaled, squares, own, w_out)
    return blocks.transpose(1, 0, 2).reshape(tokens, members * out_columns)


def on_device(hidden, in_gain, w_in, attn_gain, w_out, slope_index):
    members = lax.axis_size("heads")
    position = lax.axis_index("heads")
    shard_rows = w_in.shape[1]
    columns = attn_gain.shape[1]
    heads_local = slope_index.shape[1]
    head_width = columns // heads_local
    out_columns = w_out.shape[2]
    widened = hidden.astype(jnp.float32)
    tokens = widened.shape[0]

    scale = lax.rsqrt(jnp.mean(widened * widened, axis=1, keepdims=True) + 1e-06)
    own_hidden = lax.dynamic_slice_in_dim(hidden, position * shard_rows, shard_rows, 1)
    own_gain = lax.dynamic_slice_in_dim(in_gain, position * shard_rows, shard_rows, 1)
    normed = (own_hidden.astype(jnp.float32) * scale * own_gain).astype(jnp.bfloat16)

    proj = project(members, columns, normed, w_in[0])

    query = jax.nn.silu(proj[0]).astype(jnp.bfloat16).reshape(tokens, heads_local, head_width)
    keys = jax.nn.silu(proj[1]).astype(jnp.bfloat16).reshape(tokens, heads_local, head_width)
    values = jax.nn.silu(proj[2]).astype(jnp.bfloat16).reshape(tokens, heads_local, head_width)
    gate = proj[3]
    slopes = jnp.exp2(-0.5 * slope_index[0].astype(jnp.float32))
    positions = jnp.arange(tokens, dtype=jnp.int32)
    offset = (positions[:, None] - positions[None, :]).astype(jnp.float32)
    decay = jnp.where(
        offset[None] >= 0.0, jnp.exp(-slopes[:, None, None] * jnp.maximum(offset, 0.0)[None]), 0.0
    )
    scores = jnp.einsum("thd,shd->hts", query, keys, preferred_element_type=jnp.float32)
    weights = (scores * decay).astype(jnp.bfloat16)
    attn = jnp.einsum("hts,shd->thd", weights, values, preferred_element_type=jnp.float32).reshape(
        tokens, columns
    )
    squares = jnp.broadcast_to(jnp.sum(attn * attn, axis=1)[None, :], (8, tokens))
    scaled = attn * attn_gain[0][None, :] * jax.nn.sigmoid(gate)

    own = lax.dynamic_slice_in_dim(hidden, position * out_columns, out_columns, 1)
    return output_rows(members, scaled, squares, own, w_out[0])


def solution(mesh):
    placed = (
        P("groups", None),
        P(),
        P(None, "heads", None),
        P(None, "heads"),
        P(None, None, "heads"),
        P(None, "heads"),
    )
    return jax.shard_map(
        on_device, mesh=mesh, in_specs=placed, out_specs=P("groups", None), check_vma=False
    )
```

```python
import functools

import jax
import jax.numpy as jnp
from jax import lax
from jax.experimental import pallas as pl
from jax.experimental.pallas import tpu as pltpu
from jax.sharding import PartitionSpec as P

KINDS = 4
W_PARTS = 4
HALVES = 2


def bit_orders(steps):
    forward = tuple(range(steps))
    turned = (0,) + tuple(range(2, steps)) + (1,)
    return (forward, turned, forward, forward)


def plan(steps):
    orders = bit_orders(steps)
    depth = {"core": 8, "y": 2, "z": 3}
    free = dict.fromkeys(depth, 0.0)
    flying = dict.fromkeys(depth, 0)
    ready = {link: [] for link in depth}
    landing = []
    ops = []
    now = 3.0
    todo = list(range(KINDS))

    def link_of(unit, step):
        return ("core", "y")[orders[unit // HALVES][step]] if orders[unit // HALVES][step] < 2 else "z"

    def launch(link):
        while ready[link] and flying[link] < depth[link]:
            unit, step = ready[link].pop(0)
            bit = orders[unit // HALVES][step]
            length = (1.6 if bit == 0 else 17.4 * max(1, bit - 1)) / (1 << step)
            free[link] = max(free[link], now) + length
            flying[link] += 1
            landing.append((free[link] + 1.5, unit, step))
            ops.append(("send", unit, step))

    while todo or landing:
        landing.sort()
        if landing and (landing[0][0] <= now or not todo):
            when, unit, step = landing.pop(0)
            now = max(now, when)
            link = link_of(unit, step)
            flying[link] -= 1
            ops.append(("arrive", unit, step))
            launch(link)
            ops.append(("add", unit, step))
            now += 0.2 + 1.2 / (1 << step)
            if step + 1 < steps:
                ready[link_of(unit, step + 1)].append((unit, step + 1))
                launch(link_of(unit, step + 1))
        else:
            kind = todo.pop(0)
            ops.append(("multiply", kind))
            now += 2.6
            ready["core"] += [(kind * HALVES + half, 0) for half in range(HALVES)]
            launch("core")
    return ops


def project_kernel(members, normed_ref, w_ref, out_ref, w_buf, part, got, w_sem, send_sem, recv_sem):
    me = lax.axis_index("heads")
    steps = members.bit_length() - 1
    columns = out_ref.shape[2]
    orders = bit_orders(steps)
    width = members * columns

    def my_bit(bit):
        return lax.rem(me // (1 << bit), 2)

    def partner(bit):
        return me + (1 - 2 * my_bit(bit)) * (1 << bit)

    def w_copy(kind, piece):
        length = width // W_PARTS
        return pltpu.make_async_copy(
            w_ref.at[:, pl.ds(kind * width + piece * length, length)],
            w_buf.at[kind % 2, :, pl.ds(piece * length, length)],
            w_sem.at[kind, piece],
        )

    def w_start(kind):
        for piece in range(W_PARTS):
            w_copy(kind, piece).start()

    w_start(0)
    w_start(1)

    barrier = pltpu.get_barrier_semaphore()
    for bit in range(steps):
        pl.semaphore_signal(barrier, inc=1, device_id={"heads": partner(bit)})
    pl.semaphore_wait(barrier, steps)

    def multiply(kind):
        for piece in range(W_PARTS):
            w_copy(kind, piece).wait()

        @pl.loop(0, members)
        def _(place):
            owner = 0
            for step, bit in enumerate(orders[kind]):
                owner = owner + lax.rem(place // (1 << (steps - 1 - step)), 2) * (1 << bit)
            begin = pl.multiple_of(owner * columns, columns)
            block = jnp.dot(
                normed_ref[...],
                w_buf[kind % 2, :, pl.ds(begin, columns)],
                preferred_element_type=jnp.float32,
            )
            part[kind, place] = block.astype(part.dtype)

        if kind + 2 < KINDS:
            w_start(kind + 2)

    def layout(kind, step):
        base = 0
        for earlier in range(step):
            base = base + my_bit(orders[kind][earlier]) * (members >> (earlier + 1))
        length = members >> (step + 1)
        bit = orders[kind][step]
        keep = base + my_bit(bit) * length
        give = base + (1 - my_bit(bit)) * length
        return length, keep, give, members - (members >> step)

    half_rows = out_ref.shape[1] // HALVES

    def rows_of(unit):
        return pl.ds(unit % HALVES * half_rows, half_rows)

    def remote(unit, step):
        kind = unit // HALVES
        length, _, give, at = layout(kind, step)
        return pltpu.make_async_remote_copy(
            src_ref=part.at[kind, pl.ds(give, length), rows_of(unit)],
            dst_ref=got.at[kind, pl.ds(at, length), rows_of(unit)],
            send_sem=send_sem.at[unit, step],
            recv_sem=recv_sem.at[unit, step],
            device_id={"heads": partner(orders[kind][step])},
        )

    def add(unit, step):
        kind, rows = unit // HALVES, rows_of(unit)
        length, keep, _, at = layout(kind, step)
        if length == 1:
            out_ref[kind, rows] = part[kind, keep, rows].astype(jnp.float32) + got[
                kind, at, rows
            ].astype(jnp.float32)
            return

        @pl.loop(0, length)
        def _(index):
            total = part[kind, keep + index, rows].astype(jnp.float32) + got[
                kind, at + index, rows
            ].astype(jnp.float32)
            part[kind, keep + index, rows] = total.astype(part.dtype)

    for name, *where in plan(steps):
        if name == "multiply":
            multiply(*where)
        elif name == "send":
            remote(*where).start()
        elif name == "arrive":
            remote(*where).wait_recv()
        else:
            add(*where)
    for unit in range(KINDS * HALVES):
        for step in range(steps):
            remote(unit, step).wait_send()


def project(members, columns, normed, w_in):
    tokens, rows = normed.shape
    steps = members.bit_length() - 1
    return pl.pallas_call(
        functools.partial(project_kernel, members),
        out_shape=jax.ShapeDtypeStruct((KINDS, tokens, columns), jnp.float32),
        in_specs=[
            pl.BlockSpec(memory_space=pltpu.VMEM),
            pl.BlockSpec(memory_space=pl.ANY),
        ],
        out_specs=pl.BlockSpec(memory_space=pltpu.VMEM),
        scratch_shapes=[
            pltpu.VMEM((2, rows, members * columns), jnp.bfloat16),
            pltpu.VMEM((KINDS, members, tokens, columns), jnp.bfloat16),
            pltpu.VMEM((KINDS, members - 1, tokens, columns), jnp.bfloat16),
            pltpu.SemaphoreType.DMA((KINDS, W_PARTS)),
            pltpu.SemaphoreType.DMA((KINDS * HALVES, steps)),
            pltpu.SemaphoreType.DMA((KINDS * HALVES, steps)),
        ],
        compiler_params=pltpu.CompilerParams(
            collective_id=0, has_side_effects=True, vmem_limit_bytes=56 * 1024 * 1024
        ),
        cost_estimate=pl.CostEstimate(
            flops=2 * tokens * rows * KINDS * members * columns,
            bytes_accessed=2 * rows * KINDS * members * columns,
            transcendentals=0,
        ),
    )(normed, w_in)


def output_kernel(
    members, attn_width, scaled_ref, squares_ref, own_ref, w_ref, out_ref,
    w_buf, mix, acc, res, tot, tot_got, w_sem, tot_sem, mix_send, mix_recv, res_send, res_recv,
):
    me = lax.axis_index("heads")
    steps = members.bit_length() - 1
    halves, _, tokens, half = mix.shape
    columns = scaled_ref.shape[1]
    res_rows = res.shape[2]
    far_bits = tuple(range(steps - 1, 1, -1))
    orders = (far_bits + (1, 0), (1,) + far_bits + (0,))

    def my_bit(bit):
        return lax.rem(me // (1 << bit), 2)

    def partner(bit):
        return me + (1 - 2 * my_bit(bit)) * (1 << bit)

    w_rows = w_ref.shape[0] // W_PARTS

    def w_copy(piece):
        rows = pl.ds(piece * w_rows, w_rows)
        return pltpu.make_async_copy(w_ref.at[rows], w_buf.at[rows], w_sem.at[piece])

    for piece in range(W_PARTS):
        w_copy(piece).start()

    barrier = pltpu.get_barrier_semaphore()
    for bit in range(steps):
        pl.semaphore_signal(barrier, inc=1, device_id={"heads": partner(bit)})
    pl.semaphore_wait(barrier, steps)

    def total_copy(step):
        return pltpu.make_async_remote_copy(
            src_ref=tot.at[step],
            dst_ref=tot_got.at[step],
            send_sem=tot_sem.at[0, step],
            recv_sem=tot_sem.at[1, step],
            device_id={"heads": partner(step)},
        )

    tot[0] = squares_ref[...]
    for step in range(steps):
        total_copy(step).start()
        total_copy(step).wait_recv()
        tot[step + 1] = tot[step] + tot_got[step]
    across = jnp.broadcast_to(tot[steps][:1], (tokens, tokens))
    diagonal = lax.broadcasted_iota(jnp.int32, (tokens, tokens), 0) == lax.broadcasted_iota(
        jnp.int32, (tokens, tokens), 1
    )
    total = jnp.sum(jnp.where(diagonal, across, 0.0), axis=1, keepdims=True)
    norm = lax.rsqrt(total / attn_width + 1e-06)

    def held(order, step):
        base = 0
        for later in range(step, steps):
            base = base + my_bit(order[later]) * (1 << later)
        return base

    def incoming(order, step):
        return held(order, step) + (1 - 2 * my_bit(order[step])) * (1 << step)

    def owner_of(order, place):
        owner = 0
        for step, bit in enumerate(order):
            owner = owner + lax.rem(place // (1 << step), 2) * (1 << bit)
        return owner

    def block_copy(buffer, sends, recvs, which, step, base):
        run = pl.ds(base, 1 << step)
        return pltpu.make_async_remote_copy(
            src_ref=buffer.at[which, run],
            dst_ref=buffer.at[which, run],
            send_sem=sends.at[which, step],
            recv_sem=recvs.at[which, step],
            device_id={"heads": partner(orders[which][step])},
        )

    def mix_start(which, step):
        block_copy(mix, mix_send, mix_recv, which, step, held(orders[which], step)).start()

    def mix_arrive(which, step):
        block_copy(mix, mix_send, mix_recv, which, step, incoming(orders[which], step)).wait_recv()

    def res_start(which, step):
        block_copy(res, res_send, res_recv, which, step, held(orders[which], step)).start()

    def res_arrive(which, step):
        block_copy(res, res_send, res_recv, which, step, incoming(orders[which], step)).wait_recv()

    def multiply(which, first, count):
        @pl.loop(0, count)
        def _(index):
            place = first + index
            begin = pl.multiple_of(owner_of(orders[which], place) * columns + which * half, half)
            acc[...] += jnp.dot(
                mix[which, place], w_buf[pl.ds(begin, half)], preferred_element_type=jnp.float32
            )

    for which in range(halves):
        lanes = slice(which * half, (which + 1) * half)
        mix[which, held(orders[which], 0)] = (scaled_ref[:, lanes] * norm).astype(mix.dtype)
        mix_start(which, 0)
    acc[...] = own_ref[...].astype(jnp.float32)
    for piece in range(W_PARTS):
        w_copy(piece).wait()
    for which in range(halves):
        multiply(which, held(orders[which], 0), 1)
    for step in range(steps):
        for which in range(halves):
            mix_arrive(which, step)
            if step + 1 < steps:
                mix_start(which, step + 1)
            multiply(which, incoming(orders[which], step), 1 << step)

    for which in range(2):
        rows = slice(which * res_rows, (which + 1) * res_rows)
        res[which, held(orders[which], 0)] = acc[rows].astype(res.dtype)
        res_start(which, 0)

    def put(which, first, count):
        @pl.loop(0, count)
        def _(index):
            place = first + index
            rows = slice(which * res_rows, (which + 1) * res_rows)
            out_ref[owner_of(orders[which], place), rows] = res[which, place]

    for which in range(2):
        put(which, held(orders[which], 0), 1)
    for step in range(steps):
        for which in range(2):
            res_arrive(which, step)
            if step + 1 < steps:
                res_start(which, step + 1)
            put(which, incoming(orders[which], step), 1 << step)

    for step in range(steps):
        total_copy(step).wait_send()
        for which in range(halves):
            block_copy(mix, mix_send, mix_recv, which, step, held(orders[which], step)).wait_send()
        for which in range(2):
            block_copy(res, res_send, res_recv, which, step, held(orders[which], step)).wait_send()


def output_rows(members, scaled, squares, own, w_out):
    tokens, columns = scaled.shape
    out_columns = own.shape[1]
    steps = members.bit_length() - 1
    halves = 2 if columns % 256 == 0 else 1
    whole = pl.BlockSpec(memory_space=pltpu.VMEM)
    blocks = pl.pallas_call(
        functools.partial(output_kernel, members, columns * members),
        out_shape=jax.ShapeDtypeStruct((members, tokens, out_columns), jnp.bfloat16),
        in_specs=[whole, whole, whole, pl.BlockSpec(memory_space=pl.ANY)],
        out_specs=whole,
        scratch_shapes=[
            pltpu.VMEM(w_out.shape, jnp.bfloat16),
            pltpu.VMEM((halves, members, tokens, columns // halves), jnp.bfloat16),
            pltpu.VMEM((tokens, out_columns), jnp.float32),
            pltpu.VMEM((2, members, tokens // 2, out_columns), jnp.bfloat16),
            pltpu.VMEM((steps + 1,) + squares.shape, jnp.float32),
            pltpu.VMEM((steps,) + squares.shape, jnp.float32),
            pltpu.SemaphoreType.DMA((W_PARTS,)),
            pltpu.SemaphoreType.DMA((2, steps)),
            pltpu.SemaphoreType.DMA((halves, steps)),
            pltpu.SemaphoreType.DMA((halves, steps)),
            pltpu.SemaphoreType.DMA((2, steps)),
            pltpu.SemaphoreType.DMA((2, steps)),
        ],
        compiler_params=pltpu.CompilerParams(
            collective_id=1, has_side_effects=True, vmem_limit_bytes=48 * 1024 * 1024
        ),
        cost_estimate=pl.CostEstimate(
            flops=2 * tokens * w_out.shape[0] * out_columns,
            bytes_accessed=2 * w_out.shape[0] * out_columns,
            transcendentals=0,
        ),
    )(scaled, squares, own, w_out)
    return blocks.transpose(1, 0, 2).reshape(tokens, members * out_columns)


def on_device(hidden, in_gain, w_in, attn_gain, w_out, slope_index):
    members = lax.axis_size("heads")
    position = lax.axis_index("heads")
    shard_rows = w_in.shape[1]
    columns = attn_gain.shape[1]
    heads_local = slope_index.shape[1]
    head_width = columns // heads_local
    out_columns = w_out.shape[2]
    widened = hidden.astype(jnp.float32)
    tokens = widened.shape[0]

    scale = lax.rsqrt(jnp.mean(widened * widened, axis=1, keepdims=True) + 1e-06)
    own_hidden = lax.dynamic_slice_in_dim(hidden, position * shard_rows, shard_rows, 1)
    own_gain = lax.dynamic_slice_in_dim(in_gain, position * shard_rows, shard_rows, 1)
    normed = (own_hidden.astype(jnp.float32) * scale * own_gain).astype(jnp.bfloat16)

    proj = project(members, columns, normed, w_in[0])

    query = jax.nn.silu(proj[0]).astype(jnp.bfloat16).reshape(tokens, heads_local, head_width)
    keys = jax.nn.silu(proj[1]).astype(jnp.bfloat16).reshape(tokens, heads_local, head_width)
    values = jax.nn.silu(proj[2]).astype(jnp.bfloat16).reshape(tokens, heads_local, head_width)
    gate = proj[3]
    slopes = jnp.exp2(-0.5 * slope_index[0].astype(jnp.float32))
    positions = jnp.arange(tokens, dtype=jnp.int32)
    offset = (positions[:, None] - positions[None, :]).astype(jnp.float32)
    decay = jnp.where(
        offset[None] >= 0.0, jnp.exp(-slopes[:, None, None] * jnp.maximum(offset, 0.0)[None]), 0.0
    )
    scores = jnp.einsum("thd,shd->hts", query, keys, preferred_element_type=jnp.float32)
    weights = (scores * decay).astype(jnp.bfloat16)
    attn = jnp.einsum("hts,shd->thd", weights, values, preferred_element_type=jnp.float32).reshape(
        tokens, columns
    )
    squares = jnp.broadcast_to(jnp.sum(attn * attn, axis=1)[None, :], (8, tokens))
    scaled = attn * attn_gain[0][None, :] * jax.nn.sigmoid(gate)

    own = lax.dynamic_slice_in_dim(hidden, position * out_columns, out_columns, 1)
    return output_rows(members, scaled, squares, own, w_out[0])


def solution(mesh):
    placed = (
        P("groups", None),
        P(),
        P(None, "heads", None),
        P(None, "heads"),
        P(None, None, "heads"),
        P(None, "heads"),
    )
    return jax.shard_map(
        on_device, mesh=mesh, in_specs=placed, out_specs=P("groups", None), check_vma=False
    )
```

```python
import functools

import jax
import jax.numpy as jnp
from jax import lax
from jax.experimental import pallas as pl
from jax.experimental.pallas import tpu as pltpu
from jax.sharding import PartitionSpec as P

KINDS = 4
W_PARTS = 4
HALVES = 2
TURNED = (1, 3)


def bit_orders(steps):
    forward = tuple(range(steps))
    turned = (0,) + tuple(range(2, steps)) + (1,)
    return tuple(turned if unit in TURNED else forward for unit in range(KINDS * HALVES))


def plan(steps):
    orders = bit_orders(steps)
    depth = {"core": 8, "y": 2, "near": 2, "far": 2}
    free = dict.fromkeys(depth, 0.0)
    flying = dict.fromkeys(depth, 0)
    ready = {link: [] for link in depth}
    landing = []
    ops = []
    now = 3.0
    todo = list(range(KINDS))

    def link_of(unit, step):
        return ("core", "y", "near", "far")[min(orders[unit][step], 3)]

    def launch(link):
        while ready[link] and flying[link] < depth[link]:
            unit, step = ready[link].pop(0)
            bit = orders[unit][step]
            length = (1.6 if bit == 0 else 17.4 * max(1, bit - 1)) / (1 << step)
            free[link] = max(free[link], now) + length
            flying[link] += 1
            landing.append((free[link] + 1.5, unit, step))
            ops.append(("send", unit, step))

    while todo or landing:
        landing.sort()
        if landing and (landing[0][0] <= now or not todo):
            when, unit, step = landing.pop(0)
            now = max(now, when)
            link = link_of(unit, step)
            flying[link] -= 1
            ops.append(("arrive", unit, step))
            launch(link)
            ops.append(("add", unit, step))
            now += 0.1 + 0.7 / (1 << step)
            if step + 1 < steps:
                ready[link_of(unit, step + 1)].append((unit, step + 1))
                launch(link_of(unit, step + 1))
        else:
            kind = todo.pop(0)
            ops.append(("multiply", kind))
            now += 5.5
            ready["core"] += [(kind * HALVES + half, 0) for half in range(HALVES)]
            launch("core")
    return ops


def project_kernel(members, normed_ref, w_ref, out_ref, w_buf, part, got, w_sem, send_sem, recv_sem):
    me = lax.axis_index("heads")
    steps = members.bit_length() - 1
    columns = out_ref.shape[2]
    orders = bit_orders(steps)
    half_rows = out_ref.shape[1] // HALVES
    width = members * columns

    def my_bit(bit):
        return lax.rem(me // (1 << bit), 2)

    def partner(bit):
        return me + (1 - 2 * my_bit(bit)) * (1 << bit)

    def w_copy(kind, piece):
        length = width // W_PARTS
        return pltpu.make_async_copy(
            w_ref.at[:, pl.ds(kind * width + piece * length, length)],
            w_buf.at[kind % 2, :, pl.ds(piece * length, length)],
            w_sem.at[kind, piece],
        )

    def w_start(kind):
        for piece in range(W_PARTS):
            w_copy(kind, piece).start()

    w_start(0)
    w_start(1)

    barrier = pltpu.get_barrier_semaphore()
    for bit in range(steps):
        pl.semaphore_signal(barrier, inc=1, device_id={"heads": partner(bit)})
    pl.semaphore_wait(barrier, steps)

    def multiply(kind):
        for piece in range(W_PARTS):
            w_copy(kind, piece).wait()

        @pl.loop(0, members)
        def _(owner):
            begin = pl.multiple_of(owner * columns, columns)
            block = jnp.dot(
                normed_ref[...],
                w_buf[kind % 2, :, pl.ds(begin, columns)],
                preferred_element_type=jnp.float32,
            ).astype(part.dtype)
            for half in range(HALVES):
                place = 0
                for step, bit in enumerate(orders[kind * HALVES + half]):
                    place = place + lax.rem(owner // (1 << bit), 2) * (members >> (step + 1))
                rows = slice(half * half_rows, (half + 1) * half_rows)
                part[kind, place, rows] = block[rows]

        if kind + 2 < KINDS:
            w_start(kind + 2)

    def layout(unit, step):
        base = 0
        for earlier in range(step):
            base = base + my_bit(orders[unit][earlier]) * (members >> (earlier + 1))
        length = members >> (step + 1)
        bit = orders[unit][step]
        keep = base + my_bit(bit) * length
        give = base + (1 - my_bit(bit)) * length
        return length, keep, give, members - (members >> step)

    def rows_of(unit):
        return pl.ds(unit % HALVES * half_rows, half_rows)

    def remote(unit, step):
        kind = unit // HALVES
        length, _, give, at = layout(unit, step)
        return pltpu.make_async_remote_copy(
            src_ref=part.at[kind, pl.ds(give, length), rows_of(unit)],
            dst_ref=got.at[kind, pl.ds(at, length), rows_of(unit)],
            send_sem=send_sem.at[unit, step],
            recv_sem=recv_sem.at[unit, step],
            device_id={"heads": partner(orders[unit][step])},
        )

    def add(unit, step):
        kind, rows = unit // HALVES, rows_of(unit)
        length, keep, _, at = layout(unit, step)
        if length == 1:
            out_ref[kind, rows] = part[kind, keep, rows].astype(jnp.float32) + got[
                kind, at, rows
            ].astype(jnp.float32)
            return

        @pl.loop(0, length)
        def _(index):
            total = part[kind, keep + index, rows].astype(jnp.float32) + got[
                kind, at + index, rows
            ].astype(jnp.float32)
            part[kind, keep + index, rows] = total.astype(part.dtype)

    for name, *where in plan(steps):
        if name == "multiply":
            multiply(*where)
        elif name == "send":
            remote(*where).start()
        elif name == "arrive":
            remote(*where).wait_recv()
        else:
            add(*where)
    for unit in range(KINDS * HALVES):
        for step in range(steps):
            remote(unit, step).wait_send()


def project(members, columns, normed, w_in):
    tokens, rows = normed.shape
    steps = members.bit_length() - 1
    return pl.pallas_call(
        functools.partial(project_kernel, members),
        out_shape=jax.ShapeDtypeStruct((KINDS, tokens, columns), jnp.float32),
        in_specs=[
            pl.BlockSpec(memory_space=pltpu.VMEM),
            pl.BlockSpec(memory_space=pl.ANY),
        ],
        out_specs=pl.BlockSpec(memory_space=pltpu.VMEM),
        scratch_shapes=[
            pltpu.VMEM((2, rows, members * columns), jnp.bfloat16),
            pltpu.VMEM((KINDS, members, tokens, columns), jnp.bfloat16),
            pltpu.VMEM((KINDS, members - 1, tokens, columns), jnp.bfloat16),
            pltpu.SemaphoreType.DMA((KINDS, W_PARTS)),
            pltpu.SemaphoreType.DMA((KINDS * HALVES, steps)),
            pltpu.SemaphoreType.DMA((KINDS * HALVES, steps)),
        ],
        compiler_params=pltpu.CompilerParams(
            collective_id=0, has_side_effects=True, vmem_limit_bytes=56 * 1024 * 1024
        ),
        cost_estimate=pl.CostEstimate(
            flops=2 * tokens * rows * KINDS * members * columns,
            bytes_accessed=2 * rows * KINDS * members * columns,
            transcendentals=0,
        ),
    )(normed, w_in)


def output_kernel(
    members, attn_width, scaled_ref, squares_ref, own_ref, w_ref, out_ref,
    w_buf, mix, acc, res, tot, tot_got, w_sem, tot_sem, mix_send, mix_recv, res_send, res_recv,
):
    me = lax.axis_index("heads")
    steps = members.bit_length() - 1
    halves, _, tokens, half = mix.shape
    columns = scaled_ref.shape[1]
    res_rows = res.shape[2]
    far_bits = tuple(range(steps - 1, 1, -1))
    orders = (far_bits + (1, 0), (1,) + far_bits + (0,))

    def my_bit(bit):
        return lax.rem(me // (1 << bit), 2)

    def partner(bit):
        return me + (1 - 2 * my_bit(bit)) * (1 << bit)

    w_rows = w_ref.shape[0] // W_PARTS

    def w_copy(piece):
        rows = pl.ds(piece * w_rows, w_rows)
        return pltpu.make_async_copy(w_ref.at[rows], w_buf.at[rows], w_sem.at[piece])

    for piece in range(W_PARTS):
        w_copy(piece).start()

    barrier = pltpu.get_barrier_semaphore()
    for bit in range(steps):
        pl.semaphore_signal(barrier, inc=1, device_id={"heads": partner(bit)})
    pl.semaphore_wait(barrier, steps)

    def total_copy(step):
        return pltpu.make_async_remote_copy(
            src_ref=tot.at[step],
            dst_ref=tot_got.at[step],
            send_sem=tot_sem.at[0, step],
            recv_sem=tot_sem.at[1, step],
            device_id={"heads": partner(step)},
        )

    tot[0] = squares_ref[...]
    for step in range(steps):
        total_copy(step).start()
        total_copy(step).wait_recv()
        tot[step + 1] = tot[step] + tot_got[step]
    across = jnp.broadcast_to(tot[steps][:1], (tokens, tokens))
    diagonal = lax.broadcasted_iota(jnp.int32, (tokens, tokens), 0) == lax.broadcasted_iota(
        jnp.int32, (tokens, tokens), 1
    )
    total = jnp.sum(jnp.where(diagonal, across, 0.0), axis=1, keepdims=True)
    norm = lax.rsqrt(total / attn_width + 1e-06)

    def held(order, step):
        base = 0
        for later in range(step, steps):
            base = base + my_bit(order[later]) * (1 << later)
        return base

    def incoming(order, step):
        return held(order, step) + (1 - 2 * my_bit(order[step])) * (1 << step)

    def owner_of(order, place):
        owner = 0
        for step, bit in enumerate(order):
            owner = owner + lax.rem(place // (1 << step), 2) * (1 << bit)
        return owner

    def block_copy(buffer, sends, recvs, which, step, base):
        run = pl.ds(base, 1 << step)
        return pltpu.make_async_remote_copy(
            src_ref=buffer.at[which, run],
            dst_ref=buffer.at[which, run],
            send_sem=sends.at[which, step],
            recv_sem=recvs.at[which, step],
            device_id={"heads": partner(orders[which][step])},
        )

    def mix_start(which, step):
        block_copy(mix, mix_send, mix_recv, which, step, held(orders[which], step)).start()

    def mix_arrive(which, step):
        block_copy(mix, mix_send, mix_recv, which, step, incoming(orders[which], step)).wait_recv()

    def res_start(which, step):
        block_copy(res, res_send, res_recv, which, step, held(orders[which], step)).start()

    def res_arrive(which, step):
        block_copy(res, res_send, res_recv, which, step, incoming(orders[which], step)).wait_recv()

    def multiply(which, first, count):
        @pl.loop(0, count)
        def _(index):
            place = first + index
            begin = pl.multiple_of(owner_of(orders[which], place) * columns + which * half, half)
            acc[...] += jnp.dot(
                mix[which, place], w_buf[pl.ds(begin, half)], preferred_element_type=jnp.float32
            )

    for which in range(halves):
        lanes = slice(which * half, (which + 1) * half)
        mix[which, held(orders[which], 0)] = (scaled_ref[:, lanes] * norm).astype(mix.dtype)
        mix_start(which, 0)
    acc[...] = own_ref[...].astype(jnp.float32)
    for piece in range(W_PARTS):
        w_copy(piece).wait()
    for which in range(halves):
        multiply(which, held(orders[which], 0), 1)
    for step in range(steps):
        for which in range(halves):
            mix_arrive(which, step)
            if step + 1 < steps:
                mix_start(which, step + 1)
            multiply(which, incoming(orders[which], step), 1 << step)

    for which in range(2):
        rows = slice(which * res_rows, (which + 1) * res_rows)
        res[which, held(orders[which], 0)] = acc[rows].astype(res.dtype)
        res_start(which, 0)

    def put(which, first, count):
        @pl.loop(0, count)
        def _(index):
            place = first + index
            rows = slice(which * res_rows, (which + 1) * res_rows)
            out_ref[owner_of(orders[which], place), rows] = res[which, place]

    for which in range(2):
        put(which, held(orders[which], 0), 1)
    for step in range(steps):
        for which in range(2):
            res_arrive(which, step)
            if step + 1 < steps:
                res_start(which, step + 1)
            put(which, incoming(orders[which], step), 1 << step)

    for step in range(steps):
        total_copy(step).wait_send()
        for which in range(halves):
            block_copy(mix, mix_send, mix_recv, which, step, held(orders[which], step)).wait_send()
        for which in range(2):
            block_copy(res, res_send, res_recv, which, step, held(orders[which], step)).wait_send()


def output_rows(members, scaled, squares, own, w_out):
    tokens, columns = scaled.shape
    out_columns = own.shape[1]
    steps = members.bit_length() - 1
    halves = 2 if columns % 256 == 0 else 1
    whole = pl.BlockSpec(memory_space=pltpu.VMEM)
    blocks = pl.pallas_call(
        functools.partial(output_kernel, members, columns * members),
        out_shape=jax.ShapeDtypeStruct((members, tokens, out_columns), jnp.bfloat16),
        in_specs=[whole, whole, whole, pl.BlockSpec(memory_space=pl.ANY)],
        out_specs=whole,
        scratch_shapes=[
            pltpu.VMEM(w_out.shape, jnp.bfloat16),
            pltpu.VMEM((halves, members, tokens, columns // halves), jnp.bfloat16),
            pltpu.VMEM((tokens, out_columns), jnp.float32),
            pltpu.VMEM((2, members, tokens // 2, out_columns), jnp.bfloat16),
            pltpu.VMEM((steps + 1,) + squares.shape, jnp.float32),
            pltpu.VMEM((steps,) + squares.shape, jnp.float32),
            pltpu.SemaphoreType.DMA((W_PARTS,)),
            pltpu.SemaphoreType.DMA((2, steps)),
            pltpu.SemaphoreType.DMA((halves, steps)),
            pltpu.SemaphoreType.DMA((halves, steps)),
            pltpu.SemaphoreType.DMA((2, steps)),
            pltpu.SemaphoreType.DMA((2, steps)),
        ],
        compiler_params=pltpu.CompilerParams(
            collective_id=1, has_side_effects=True, vmem_limit_bytes=48 * 1024 * 1024
        ),
        cost_estimate=pl.CostEstimate(
            flops=2 * tokens * w_out.shape[0] * out_columns,
            bytes_accessed=2 * w_out.shape[0] * out_columns,
            transcendentals=0,
        ),
    )(scaled, squares, own, w_out)
    return blocks.transpose(1, 0, 2).reshape(tokens, members * out_columns)


def on_device(hidden, in_gain, w_in, attn_gain, w_out, slope_index):
    members = lax.axis_size("heads")
    position = lax.axis_index("heads")
    shard_rows = w_in.shape[1]
    columns = attn_gain.shape[1]
    heads_local = slope_index.shape[1]
    head_width = columns // heads_local
    out_columns = w_out.shape[2]
    widened = hidden.astype(jnp.float32)
    tokens = widened.shape[0]

    scale = lax.rsqrt(jnp.mean(widened * widened, axis=1, keepdims=True) + 1e-06)
    own_hidden = lax.dynamic_slice_in_dim(hidden, position * shard_rows, shard_rows, 1)
    own_gain = lax.dynamic_slice_in_dim(in_gain, position * shard_rows, shard_rows, 1)
    normed = (own_hidden.astype(jnp.float32) * scale * own_gain).astype(jnp.bfloat16)

    proj = project(members, columns, normed, w_in[0])

    query = jax.nn.silu(proj[0]).astype(jnp.bfloat16).reshape(tokens, heads_local, head_width)
    keys = jax.nn.silu(proj[1]).astype(jnp.bfloat16).reshape(tokens, heads_local, head_width)
    values = jax.nn.silu(proj[2]).astype(jnp.bfloat16).reshape(tokens, heads_local, head_width)
    gate = proj[3]
    slopes = jnp.exp2(-0.5 * slope_index[0].astype(jnp.float32))
    positions = jnp.arange(tokens, dtype=jnp.int32)
    offset = (positions[:, None] - positions[None, :]).astype(jnp.float32)
    decay = jnp.where(
        offset[None] >= 0.0, jnp.exp(-slopes[:, None, None] * jnp.maximum(offset, 0.0)[None]), 0.0
    )
    scores = jnp.einsum("thd,shd->hts", query, keys, preferred_element_type=jnp.float32)
    weights = (scores * decay).astype(jnp.bfloat16)
    attn = jnp.einsum("hts,shd->thd", weights, values, preferred_element_type=jnp.float32).reshape(
        tokens, columns
    )
    squares = jnp.broadcast_to(jnp.sum(attn * attn, axis=1)[None, :], (8, tokens))
    scaled = attn * attn_gain[0][None, :] * jax.nn.sigmoid(gate)

    own = lax.dynamic_slice_in_dim(hidden, position * out_columns, out_columns, 1)
    return output_rows(members, scaled, squares, own, w_out[0])


def solution(mesh):
    placed = (
        P("groups", None),
        P(),
        P(None, "heads", None),
        P(None, "heads"),
        P(None, None, "heads"),
        P(None, "heads"),
    )
    return jax.shard_map(
        on_device, mesh=mesh, in_specs=placed, out_specs=P("groups", None), check_vma=False
    )
```

```python
import functools

import jax
import jax.numpy as jnp
from jax import lax
from jax.experimental import pallas as pl
from jax.experimental.pallas import tpu as pltpu
from jax.sharding import PartitionSpec as P

KINDS = 4
W_PARTS = 4
HALVES = 2
TURNED = (1, 3)


def bit_orders(steps):
    forward = tuple(range(steps))
    turned = (0,) + tuple(range(2, steps)) + (1,)
    return tuple(turned if unit in TURNED else forward for unit in range(KINDS * HALVES))


def plan(steps):
    orders = bit_orders(steps)
    depth = {"core": 8, "y": 2, "near": 2, "far": 2}
    free = dict.fromkeys(depth, 0.0)
    flying = dict.fromkeys(depth, 0)
    ready = {link: [] for link in depth}
    landing = []
    ops = []
    now = 3.0
    todo = list(range(KINDS))

    def link_of(unit, step):
        return ("core", "y", "near", "far")[min(orders[unit][step], 3)]

    def launch(link):
        while ready[link] and flying[link] < depth[link]:
            unit, step = ready[link].pop(0)
            bit = orders[unit][step]
            length = (1.6 if bit == 0 else 17.4 * max(1, bit - 1)) / (1 << step)
            free[link] = max(free[link], now) + length
            flying[link] += 1
            landing.append((free[link] + 1.5, unit, step))
            ops.append(("send", unit, step))

    while todo or landing:
        landing.sort()
        if landing and (landing[0][0] <= now or not todo):
            when, unit, step = landing.pop(0)
            now = max(now, when)
            link = link_of(unit, step)
            flying[link] -= 1
            ops.append(("arrive", unit, step))
            launch(link)
            ops.append(("add", unit, step))
            now += 0.1 + 0.7 / (1 << step)
            if step + 1 < steps:
                ready[link_of(unit, step + 1)].append((unit, step + 1))
                launch(link_of(unit, step + 1))
        else:
            kind = todo.pop(0)
            ops.append(("multiply", kind))
            now += 5.5
            ready["core"] += [(kind * HALVES + half, 0) for half in range(HALVES)]
            launch("core")
    return ops


def project_kernel(members, normed_ref, w_ref, out_ref, w_buf, part, got, w_sem, send_sem, recv_sem):
    me = lax.axis_index("heads")
    steps = members.bit_length() - 1
    columns = out_ref.shape[2]
    orders = bit_orders(steps)
    half_rows = out_ref.shape[1] // HALVES
    width = members * columns

    def my_bit(bit):
        return lax.rem(me // (1 << bit), 2)

    def partner(bit):
        return me + (1 - 2 * my_bit(bit)) * (1 << bit)

    def w_copy(kind, piece):
        length = width // W_PARTS
        return pltpu.make_async_copy(
            w_ref.at[:, pl.ds(kind * width + piece * length, length)],
            w_buf.at[kind % 2, :, pl.ds(piece * length, length)],
            w_sem.at[kind, piece],
        )

    def w_start(kind):
        for piece in range(W_PARTS):
            w_copy(kind, piece).start()

    w_start(0)
    w_start(1)

    barrier = pltpu.get_barrier_semaphore()
    for bit in range(steps):
        pl.semaphore_signal(barrier, inc=1, device_id={"heads": partner(bit)})
    pl.semaphore_wait(barrier, steps)

    def multiply(kind):
        for piece in range(W_PARTS):
            w_copy(kind, piece).wait()

        @pl.loop(0, members)
        def _(owner):
            begin = pl.multiple_of(owner * columns, columns)
            block = jnp.dot(
                normed_ref[...],
                w_buf[kind % 2, :, pl.ds(begin, columns)],
                preferred_element_type=jnp.float32,
            ).astype(part.dtype)
            for half in range(HALVES):
                place = 0
                for step, bit in enumerate(orders[kind * HALVES + half]):
                    place = place + lax.rem(owner // (1 << bit), 2) * (members >> (step + 1))
                rows = slice(half * half_rows, (half + 1) * half_rows)
                part[kind, place, rows] = block[rows]

        if kind + 2 < KINDS:
            w_start(kind + 2)

    def layout(unit, step):
        base = 0
        for earlier in range(step):
            base = base + my_bit(orders[unit][earlier]) * (members >> (earlier + 1))
        length = members >> (step + 1)
        bit = orders[unit][step]
        keep = base + my_bit(bit) * length
        give = base + (1 - my_bit(bit)) * length
        return length, keep, give, members - (members >> step)

    def rows_of(unit):
        return pl.ds(unit % HALVES * half_rows, half_rows)

    def remote(unit, step):
        kind = unit // HALVES
        length, _, give, at = layout(unit, step)
        return pltpu.make_async_remote_copy(
            src_ref=part.at[kind, pl.ds(give, length), rows_of(unit)],
            dst_ref=got.at[kind, pl.ds(at, length), rows_of(unit)],
            send_sem=send_sem.at[unit, step],
            recv_sem=recv_sem.at[unit, step],
            device_id={"heads": partner(orders[unit][step])},
        )

    def add(unit, step):
        kind, rows = unit // HALVES, rows_of(unit)
        length, keep, _, at = layout(unit, step)
        if length == 1:
            out_ref[kind, rows] = part[kind, keep, rows].astype(jnp.float32) + got[
                kind, at, rows
            ].astype(jnp.float32)
            return

        @pl.loop(0, length)
        def _(index):
            total = part[kind, keep + index, rows].astype(jnp.float32) + got[
                kind, at + index, rows
            ].astype(jnp.float32)
            part[kind, keep + index, rows] = total.astype(part.dtype)

    for name, *where in plan(steps):
        if name == "multiply":
            multiply(*where)
        elif name == "send":
            remote(*where).start()
        elif name == "arrive":
            remote(*where).wait_recv()
        else:
            add(*where)
    for unit in range(KINDS * HALVES):
        for step in range(steps):
            remote(unit, step).wait_send()


def project(members, columns, normed, w_in):
    tokens, rows = normed.shape
    steps = members.bit_length() - 1
    return pl.pallas_call(
        functools.partial(project_kernel, members),
        out_shape=jax.ShapeDtypeStruct((KINDS, tokens, columns), jnp.float32),
        in_specs=[
            pl.BlockSpec(memory_space=pltpu.VMEM),
            pl.BlockSpec(memory_space=pl.ANY),
        ],
        out_specs=pl.BlockSpec(memory_space=pltpu.VMEM),
        scratch_shapes=[
            pltpu.VMEM((2, rows, members * columns), jnp.bfloat16),
            pltpu.VMEM((KINDS, members, tokens, columns), jnp.bfloat16),
            pltpu.VMEM((KINDS, members - 1, tokens, columns), jnp.bfloat16),
            pltpu.SemaphoreType.DMA((KINDS, W_PARTS)),
            pltpu.SemaphoreType.DMA((KINDS * HALVES, steps)),
            pltpu.SemaphoreType.DMA((KINDS * HALVES, steps)),
        ],
        compiler_params=pltpu.CompilerParams(
            collective_id=0, has_side_effects=True, vmem_limit_bytes=56 * 1024 * 1024
        ),
        cost_estimate=pl.CostEstimate(
            flops=2 * tokens * rows * KINDS * members * columns,
            bytes_accessed=2 * rows * KINDS * members * columns,
            transcendentals=0,
        ),
    )(normed, w_in)


def output_kernel(
    members, attn_width, scaled_ref, squares_ref, own_ref, w_ref, out_ref,
    w_buf, mix, acc, res, tot, tot_got, w_sem, tot_sem, mix_send, mix_recv, res_send, res_recv,
):
    me = lax.axis_index("heads")
    steps = members.bit_length() - 1
    halves, _, tokens, half = mix.shape
    columns = scaled_ref.shape[1]
    res_rows = res.shape[2]
    far_bits = tuple(range(steps - 1, 1, -1))
    orders = (far_bits + (1, 0), (1,) + far_bits + (0,))

    def my_bit(bit):
        return lax.rem(me // (1 << bit), 2)

    def partner(bit):
        return me + (1 - 2 * my_bit(bit)) * (1 << bit)

    w_rows = w_ref.shape[0] // W_PARTS

    def w_copy(piece):
        rows = pl.ds(piece * w_rows, w_rows)
        return pltpu.make_async_copy(w_ref.at[rows], w_buf.at[rows], w_sem.at[piece])

    for piece in range(W_PARTS):
        w_copy(piece).start()

    barrier = pltpu.get_barrier_semaphore()
    for bit in range(steps):
        pl.semaphore_signal(barrier, inc=1, device_id={"heads": partner(bit)})
    pl.semaphore_wait(barrier, steps)

    def total_copy(step):
        return pltpu.make_async_remote_copy(
            src_ref=tot.at[step],
            dst_ref=tot_got.at[step],
            send_sem=tot_sem.at[0, step],
            recv_sem=tot_sem.at[1, step],
            device_id={"heads": partner(step)},
        )

    tot[0] = squares_ref[...]
    for step in range(steps):
        total_copy(step).start()
        total_copy(step).wait_recv()
        tot[step + 1] = tot[step] + tot_got[step]
    across = jnp.broadcast_to(tot[steps][:1], (tokens, tokens))
    diagonal = lax.broadcasted_iota(jnp.int32, (tokens, tokens), 0) == lax.broadcasted_iota(
        jnp.int32, (tokens, tokens), 1
    )
    total = jnp.sum(jnp.where(diagonal, across, 0.0), axis=1, keepdims=True)
    norm = lax.rsqrt(total / attn_width + 1e-06)

    def held(order, step):
        base = 0
        for later in range(step, steps):
            base = base + my_bit(order[later]) * (1 << later)
        return base

    def incoming(order, step):
        return held(order, step) + (1 - 2 * my_bit(order[step])) * (1 << step)

    def owner_of(order, place):
        owner = 0
        for step, bit in enumerate(order):
            owner = owner + lax.rem(place // (1 << step), 2) * (1 << bit)
        return owner

    def block_copy(buffer, sends, recvs, which, step, base):
        run = pl.ds(base, 1 << step)
        return pltpu.make_async_remote_copy(
            src_ref=buffer.at[which, run],
            dst_ref=buffer.at[which, run],
            send_sem=sends.at[which, step],
            recv_sem=recvs.at[which, step],
            device_id={"heads": partner(orders[which][step])},
        )

    def mix_start(which, step):
        block_copy(mix, mix_send, mix_recv, which, step, held(orders[which], step)).start()

    def mix_arrive(which, step):
        block_copy(mix, mix_send, mix_recv, which, step, incoming(orders[which], step)).wait_recv()

    def res_start(which, step):
        block_copy(res, res_send, res_recv, which, step, held(orders[which], step)).start()

    def res_arrive(which, step):
        block_copy(res, res_send, res_recv, which, step, incoming(orders[which], step)).wait_recv()

    def run_of(which, index):
        if index == 0:
            return held(orders[which], 0), 1
        return incoming(orders[which], index - 1), 1 << (index - 1)

    def sibling_run(which, index):
        base, count = run_of(which, index)
        return base + (1 - 2 * my_bit(0)) * (members // 2), count

    def core_copy(buffer, sends, recvs, which, index, base, count):
        run = pl.ds(base, count)
        return pltpu.make_async_remote_copy(
            src_ref=buffer.at[which, run],
            dst_ref=buffer.at[which, run],
            send_sem=sends.at[which, steps + index],
            recv_sem=recvs.at[which, steps + index],
            device_id={"heads": partner(0)},
        )

    def exchange(buffer, sends, recvs, pieces, start, arrive, use):
        def share(which, index):
            core_copy(buffer, sends, recvs, which, index, *run_of(which, index)).start()

        def take(which, index):
            base, count = sibling_run(which, index)
            core_copy(buffer, sends, recvs, which, index, base, count).wait_recv()
            use(which, base, count)

        for which in range(pieces):
            share(which, 0)
            use(which, *run_of(which, 0))
        for step in range(steps - 1):
            for which in range(pieces):
                arrive(which, step)
                if step + 1 < steps - 1:
                    start(which, step + 1)
                share(which, step + 1)
            for which in range(pieces):
                use(which, *run_of(which, step + 1))
                take(which, step)
        for which in range(pieces):
            take(which, steps - 1)
        for which in range(pieces):
            for step in range(steps - 1):
                base = held(orders[which], step)
                block_copy(buffer, sends, recvs, which, step, base).wait_send()
            for index in range(steps):
                core_copy(buffer, sends, recvs, which, index, *run_of(which, index)).wait_send()

    def multiply(which, first, count):
        @pl.loop(0, count)
        def _(index):
            place = first + index
            begin = pl.multiple_of(owner_of(orders[which], place) * columns + which * half, half)
            acc[...] += jnp.dot(
                mix[which, place], w_buf[pl.ds(begin, half)], preferred_element_type=jnp.float32
            )

    for which in range(halves):
        lanes = slice(which * half, (which + 1) * half)
        mix[which, held(orders[which], 0)] = (scaled_ref[:, lanes] * norm).astype(mix.dtype)
        mix_start(which, 0)
    acc[...] = own_ref[...].astype(jnp.float32)
    for piece in range(W_PARTS):
        w_copy(piece).wait()
    exchange(mix, mix_send, mix_recv, halves, mix_start, mix_arrive, multiply)

    for which in range(2):
        rows = slice(which * res_rows, (which + 1) * res_rows)
        res[which, held(orders[which], 0)] = acc[rows].astype(res.dtype)
        res_start(which, 0)

    def put(which, first, count):
        @pl.loop(0, count)
        def _(index):
            place = first + index
            rows = slice(which * res_rows, (which + 1) * res_rows)
            out_ref[owner_of(orders[which], place), rows] = res[which, place]

    exchange(res, res_send, res_recv, 2, res_start, res_arrive, put)
    for step in range(steps):
        total_copy(step).wait_send()


def output_rows(members, scaled, squares, own, w_out):
    tokens, columns = scaled.shape
    out_columns = own.shape[1]
    steps = members.bit_length() - 1
    halves = 2 if columns % 256 == 0 else 1
    whole = pl.BlockSpec(memory_space=pltpu.VMEM)
    blocks = pl.pallas_call(
        functools.partial(output_kernel, members, columns * members),
        out_shape=jax.ShapeDtypeStruct((members, tokens, out_columns), jnp.bfloat16),
        in_specs=[whole, whole, whole, pl.BlockSpec(memory_space=pl.ANY)],
        out_specs=whole,
        scratch_shapes=[
            pltpu.VMEM(w_out.shape, jnp.bfloat16),
            pltpu.VMEM((halves, members, tokens, columns // halves), jnp.bfloat16),
            pltpu.VMEM((tokens, out_columns), jnp.float32),
            pltpu.VMEM((2, members, tokens // 2, out_columns), jnp.bfloat16),
            pltpu.VMEM((steps + 1,) + squares.shape, jnp.float32),
            pltpu.VMEM((steps,) + squares.shape, jnp.float32),
            pltpu.SemaphoreType.DMA((W_PARTS,)),
            pltpu.SemaphoreType.DMA((2, steps)),
            pltpu.SemaphoreType.DMA((halves, 2 * steps)),
            pltpu.SemaphoreType.DMA((halves, 2 * steps)),
            pltpu.SemaphoreType.DMA((2, 2 * steps)),
            pltpu.SemaphoreType.DMA((2, 2 * steps)),
        ],
        compiler_params=pltpu.CompilerParams(
            collective_id=1, has_side_effects=True, vmem_limit_bytes=48 * 1024 * 1024
        ),
        cost_estimate=pl.CostEstimate(
            flops=2 * tokens * w_out.shape[0] * out_columns,
            bytes_accessed=2 * w_out.shape[0] * out_columns,
            transcendentals=0,
        ),
    )(scaled, squares, own, w_out)
    return blocks.transpose(1, 0, 2).reshape(tokens, members * out_columns)


def on_device(hidden, in_gain, w_in, attn_gain, w_out, slope_index):
    members = lax.axis_size("heads")
    position = lax.axis_index("heads")
    shard_rows = w_in.shape[1]
    columns = attn_gain.shape[1]
    heads_local = slope_index.shape[1]
    head_width = columns // heads_local
    out_columns = w_out.shape[2]
    widened = hidden.astype(jnp.float32)
    tokens = widened.shape[0]

    scale = lax.rsqrt(jnp.mean(widened * widened, axis=1, keepdims=True) + 1e-06)
    own_hidden = lax.dynamic_slice_in_dim(hidden, position * shard_rows, shard_rows, 1)
    own_gain = lax.dynamic_slice_in_dim(in_gain, position * shard_rows, shard_rows, 1)
    normed = (own_hidden.astype(jnp.float32) * scale * own_gain).astype(jnp.bfloat16)

    proj = project(members, columns, normed, w_in[0])

    query = jax.nn.silu(proj[0]).astype(jnp.bfloat16).reshape(tokens, heads_local, head_width)
    keys = jax.nn.silu(proj[1]).astype(jnp.bfloat16).reshape(tokens, heads_local, head_width)
    values = jax.nn.silu(proj[2]).astype(jnp.bfloat16).reshape(tokens, heads_local, head_width)
    gate = proj[3]
    slopes = jnp.exp2(-0.5 * slope_index[0].astype(jnp.float32))
    positions = jnp.arange(tokens, dtype=jnp.int32)
    offset = (positions[:, None] - positions[None, :]).astype(jnp.float32)
    decay = jnp.where(
        offset[None] >= 0.0, jnp.exp(-slopes[:, None, None] * jnp.maximum(offset, 0.0)[None]), 0.0
    )
    scores = jnp.einsum("thd,shd->hts", query, keys, preferred_element_type=jnp.float32)
    weights = (scores * decay).astype(jnp.bfloat16)
    attn = jnp.einsum("hts,shd->thd", weights, values, preferred_element_type=jnp.float32).reshape(
        tokens, columns
    )
    squares = jnp.broadcast_to(jnp.sum(attn * attn, axis=1)[None, :], (8, tokens))
    scaled = attn * attn_gain[0][None, :] * jax.nn.sigmoid(gate)

    own = lax.dynamic_slice_in_dim(hidden, position * out_columns, out_columns, 1)
    return output_rows(members, scaled, squares, own, w_out[0])


def solution(mesh):
    placed = (
        P("groups", None),
        P(),
        P(None, "heads", None),
        P(None, "heads"),
        P(None, None, "heads"),
        P(None, "heads"),
    )
    return jax.shard_map(
        on_device, mesh=mesh, in_specs=placed, out_specs=P("groups", None), check_vma=False
    )
```
